768 devices in a mesh: node: 64 (over z_hi, y, x), chip: 6 (over z_lo), pair: 2 (over core).
Axes of the slice: x: 4, y: 8, z: 12 (z_hi: 2, z_lo: 6; z = z_hi * 6 + z_lo), core: 2. Of those that a mesh axis runs over, the one named last changes fastest.
Arguments:
- hidden: bfloat16 [98304, 6912], P(('node', 'chip', 'pair')), may hold values from -6 to 6
- cotangent: bfloat16 [98304, 2560], P('node'), may hold values from -0.4375 to 0.4375
Outputs:
- grad_weight: float32 [2560, 6912], P('node', ('chip', 'pair'))
The draws below stay inside these ranges and needn't reach their ends.
All inputs are finite; a program needn't handle non-finite values.
Results may differ from the reference program's by a relative error of at most 0.0003.
Values may be sent and summed in bfloat16 or wider, within the bound.
No kernel may reach another device: no remote copies, remote signals or barrier semaphores. Data moves between devices by JAX's collectives and lax.ppermute only.
A program may use at most 64 MiB of HBM per device.

```python
import jax
import jax.numpy as jnp

D = 2560
FF = 6912
TOKENS = 98304


def strengthened(result, rng, source, target, parts, factor):
    def block_of(axis_at):
        return (jnp.arange(result.shape[axis_at]) // (result.shape[axis_at] // parts)).reshape((-1,) + (1,) * (result.ndim - 1 - axis_at))

    near = jax.random.permutation(rng, parts)[block_of(target)]
    second = (block_of(target) + parts // 2) % parts
    return jnp.where((block_of(source) == near) | (block_of(source) == second), factor * result, result)


def levels(stream_key, extent, pieces, smallest, largest):
    def one(dim, parts):
        draws = jax.random.uniform(jax.random.fold_in(jax.random.fold_in(stream_key, 6), dim), (parts,), jnp.float32, smallest / len(pieces), largest / len(pieces))
        return jnp.repeat(jnp.exp(draws), extent[dim] // parts).reshape((-1,) + (1,) * (len(extent) - dim - 1))

    loudness = one(*pieces[0])
    for cut in pieces[1:]:
        loudness = loudness * one(*cut)
    return loudness


def scatter_about(stream_key, shape, scale, reach, split=(), kind=jnp.bfloat16):
    gain = levels(stream_key, shape, split, -0.22, 0.18) if split else 1.0
    result = jax.random.normal(stream_key, shape, jnp.float32) * scale * gain
    return jnp.minimum(jnp.maximum(result, -reach), reach).astype(kind)


def noise_with(own_key, dims, spread, bound, pieces, heavy, kind=jnp.bfloat16):
    result = spread * jax.random.normal(own_key, dims, jnp.float32)
    if pieces:
        result = result * levels(own_key, dims, pieces, -0.22, 0.18)
    return jnp.clip(strengthened(result, jax.random.fold_in(own_key, 3), *heavy), -bound, bound).astype(kind)


def setup_inputs(seed: int = 0) -> dict:
    streams_of = jax.random.split(jax.random.key(seed), 3)
    return {
        "hidden": scatter_about(streams_of[0], (TOKENS, FF), 1.0, 6.0, ((0, 768),)),
        "cotangent": noise_with(streams_of[1], (TOKENS, D), 0.01, 0.4375, ((0, 64),), (0, 1, 64, 4.0)),
    }


def reference(hidden, cotangent):
    return jnp.dot(cotangent.T, hidden, preferred_element_type=jnp.float32)
```

```python
import jax
import jax.numpy as jnp
from jax import lax
from jax.sharding import Mesh, PartitionSpec as P

SIZES = {"zh": 2, "yh": 4, "yl": 2, "x": 4, "chip": 6, "pair": 2}
LIMIT = 60000.0


def decoded(code):
    return jnp.exp2(code)


def code_for(bound):
    e = jnp.floor(jnp.log2(LIMIT) - jnp.log2(jnp.maximum(bound, 1e-30)) - 0.01)
    return jnp.clip(e, -100.0, 100.0)


def shards(hidden, cotangent):
    t, ff = hidden.shape
    tokens, d = cotangent.shape
    groups = tokens // t
    w = ff // groups
    wide = -(-(w + 1) // 128) * 128
    near, far = SIZES["yl"] * SIZES["x"], SIZES["zh"] * SIZES["yh"]
    r = d // (near * far)

    part = lax.all_to_all(
        hidden.T.reshape(groups, w, t), ("chip", "pair"), split_axis=0, concat_axis=0, tiled=True
    )
    cot = cotangent.reshape(tokens, far, near, r).transpose(2, 1, 3, 0).reshape(d, tokens)
    top = jnp.max(jnp.abs(cotangent)).astype(jnp.float32)

    code = code_for(top * jnp.max(jnp.abs(part)).astype(jnp.float32) * tokens)
    part = part.transpose(1, 0, 2).reshape(w, tokens)
    part = jnp.pad(part, ((0, wide - w), (0, 0)))
    dims = (((1,), (1,)), ((), ()))
    lane = jnp.arange(wide) < w

    terms = lax.dot_general(cot, part, dims, preferred_element_type=jnp.float32)
    terms = jnp.where(lane, terms * decoded(code), code).astype(jnp.float16)
    got = lax.all_to_all(
        terms.reshape(near, d // near, wide), ("yl", "x"), split_axis=0, concat_axis=0, tiled=True
    )
    me = lax.axis_index(("yl", "x"))
    own = lax.dynamic_slice_in_dim(cot, me * (d // near), d // near, 0)
    own = lax.dot_general(own, part, dims, preferred_element_type=jnp.float32)
    back = decoded(-got[:, 0, w].astype(jnp.float32))
    others = (jnp.arange(near) != me)
    weight = jnp.where(others, back, 0.0)[:, None, None]
    row = (got.astype(jnp.float32) * weight).sum(0) + own

    code = code_for(LIMIT * back.sum())
    sent = jnp.where(lane, row * decoded(code), code).astype(jnp.float16)
    got = lax.all_to_all(
        sent.reshape(far, r, wide), ("zh", "yh"), split_axis=0, concat_axis=0, tiled=True
    )
    me = lax.axis_index(("zh", "yh"))
    own = lax.dynamic_slice_in_dim(row, me * r, r, 0)
    back = decoded(-got[:, 0, w].astype(jnp.float32))
    weight = jnp.where(jnp.arange(far) != me, back, 0.0)[:, None, None]
    return ((got.astype(jnp.float32) * weight).sum(0) + own)[:, :w]


def solution(mesh):
    fine = Mesh(mesh.devices.reshape(tuple(SIZES.values())), tuple(SIZES))
    node = ("zh", "yh", "yl", "x")
    in_specs = (P(node + ("chip", "pair"), None), P(node, None))
    out_specs = P(node, ("chip", "pair"))
    return jax.shard_map(shards, mesh=fine, in_specs=in_specs, out_specs=out_specs, check_vma=False)
```

```python
import jax
import jax.numpy as jnp
from jax import lax
from jax.experimental import pallas as pl
from jax.experimental.pallas import tpu as pltpu
from jax.sharding import Mesh, PartitionSpec as P

SIZES = {"zh": 2, "yh": 4, "yl": 2, "x": 4, "chip": 6, "pair": 2}
LIMIT = 60000.0
ROWS = 512


def decoded(code):
    return jnp.exp2(code)


def code_for(bound):
    e = jnp.floor(jnp.log2(LIMIT) - jnp.log2(jnp.maximum(bound, 1e-30)) - 0.01)
    return jnp.clip(e, -100.0, 100.0)


def multiply(cot_ref, part_ref, out_ref, flat):
    groups, w, t = part_ref.shape

    @pl.when(pl.program_id(0) == 0)
    def _():
        for i in range(groups):
            flat[:, i * t:(i + 1) * t] = part_ref[i]

    out_ref[:, :w] = lax.dot_general(
        cot_ref[...], flat[...], (((1,), (1,)), ((), ())), preferred_element_type=jnp.float32
    )
    out_ref[:, w:] = jnp.zeros((out_ref.shape[0], out_ref.shape[1] - w), jnp.float32)


def product(cot, part, wide):
    d, tokens = cot.shape
    groups, w, t = part.shape
    rows = min(ROWS, d)
    return pl.pallas_call(
        multiply,
        grid=(d // rows,),
        in_specs=[
            pl.BlockSpec((rows, tokens), lambda i: (i, 0)),
            pl.BlockSpec((groups, w, t), lambda i: (0, 0, 0)),
        ],
        out_specs=pl.BlockSpec((rows, wide), lambda i: (i, 0)),
        out_shape=jax.ShapeDtypeStruct((d, wide), jnp.float32),
        scratch_shapes=[pltpu.VMEM((w, tokens), jnp.bfloat16)],
        compiler_params=pltpu.CompilerParams(vmem_limit_bytes=32 * 2**20),
        cost_estimate=pl.CostEstimate(
            flops=2 * d * tokens * w, bytes_accessed=2 * d * tokens + 4 * d * wide, transcendentals=0
        ),
    )(cot, part)


def shards(hidden, cotangent):
    t, ff = hidden.shape
    tokens, d = cotangent.shape
    groups = tokens // t
    w = ff // groups
    wide = -(-(w + 1) // 128) * 128
    near, far = SIZES["yl"] * SIZES["x"], SIZES["zh"] * SIZES["yh"]
    r = d // (near * far)

    part = lax.all_to_all(
        hidden.T.reshape(groups, w, t), ("chip", "pair"), split_axis=0, concat_axis=0, tiled=True
    )
    cot = cotangent.reshape(tokens, far, near, r).transpose(2, 1, 3, 0).reshape(d, tokens)
    top = jnp.max(jnp.abs(cotangent)).astype(jnp.float32)

    code = code_for(top * jnp.max(jnp.abs(part)).astype(jnp.float32) * tokens)
    lane = jnp.arange(wide) < w

    terms = product(cot, part, wide)
    sent = jnp.where(lane, terms * decoded(code), code).astype(jnp.float16)
    got = lax.all_to_all(
        sent.reshape(near, d // near, wide), ("yl", "x"), split_axis=0, concat_axis=0, tiled=True
    )
    me = lax.axis_index(("yl", "x"))
    own = lax.dynamic_slice_in_dim(terms, me * (d // near), d // near, 0)
    back = decoded(-got[:, 0, w].astype(jnp.float32))
    others = (jnp.arange(near) != me)
    weight = jnp.where(others, back, 0.0)[:, None, None]
    row = (got.astype(jnp.float32) * weight).sum(0) + own

    code = code_for(LIMIT * back.sum())
    sent = jnp.where(lane, row * decoded(code), code).astype(jnp.float16)
    got = lax.all_to_all(
        sent.reshape(far, r, wide), ("zh", "yh"), split_axis=0, concat_axis=0, tiled=True
    )
    me = lax.axis_index(("zh", "yh"))
    own = lax.dynamic_slice_in_dim(row, me * r, r, 0)
    back = decoded(-got[:, 0, w].astype(jnp.float32))
    weight = jnp.where(jnp.arange(far) != me, back, 0.0)[:, None, None]
    return ((got.astype(jnp.float32) * weight).sum(0) + own)[:, :w]


def solution(mesh):
    fine = Mesh(mesh.devices.reshape(tuple(SIZES.values())), tuple(SIZES))
    node = ("zh", "yh", "yl", "x")
    in_specs = (P(node + ("chip", "pair"), None), P(node, None))
    out_specs = P(node, ("chip", "pair"))
    return jax.shard_map(shards, mesh=fine, in_specs=in_specs, out_specs=out_specs, check_vma=False)
```

```python
import jax
import jax.numpy as jnp
from jax import lax
from jax.experimental import pallas as pl
from jax.experimental.pallas import tpu as pltpu
from jax.sharding import Mesh, PartitionSpec as P

SIZES = {"zh": 2, "yh": 4, "yl": 2, "x": 4, "chip": 6, "pair": 2}
LIMIT = 60000.0


def decoded(code):
    return jnp.exp2(code)


def code_for(bound):
    e = jnp.floor(jnp.log2(LIMIT) - jnp.log2(jnp.maximum(bound, 1e-30)) - 0.01)
    return jnp.clip(e, -100.0, 100.0)


def multiply(me_ref, cot_ref, part_ref, out_ref, own_ref, flat):
    groups, w, t = part_ref.shape
    step, blocks = pl.program_id(0), out_ref.shape[0] // own_ref.shape[0]

    @pl.when(step == 0)
    def _():
        for i in range(groups):
            flat[:, i * t:(i + 1) * t] = part_ref[i]

    out_ref[:, :w] = lax.dot_general(
        cot_ref[...], flat[...], (((1,), (1,)), ((), ())), preferred_element_type=jnp.float32
    )
    out_ref[:, w:] = jnp.zeros((out_ref.shape[0], out_ref.shape[1] - w), jnp.float32)

    for i in range(blocks):
        @pl.when(step * blocks + i == me_ref[0])
        def _():
            own_ref[...] = out_ref[i * own_ref.shape[0]:(i + 1) * own_ref.shape[0], :]


def product(cot, part, wide, me, near):
    d, tokens = cot.shape
    groups, w, t = part.shape
    rows = 2 * (d // near)
    return pl.pallas_call(
        multiply,
        grid_spec=pltpu.PrefetchScalarGridSpec(
            num_scalar_prefetch=1,
            grid=(d // rows,),
            in_specs=[
                pl.BlockSpec((rows, tokens), lambda i, _: (i, 0)),
                pl.BlockSpec((groups, w, t), lambda i, _: (0, 0, 0)),
            ],
            out_specs=[
                pl.BlockSpec((rows, wide), lambda i, _: (i, 0)),
                pl.BlockSpec((d // near, wide), lambda i, _: (0, 0)),
            ],
            scratch_shapes=[pltpu.VMEM((w, tokens), jnp.bfloat16)],
        ),
        out_shape=[
            jax.ShapeDtypeStruct((d, wide), jnp.float32),
            jax.ShapeDtypeStruct((d // near, wide), jnp.float32),
        ],
        compiler_params=pltpu.CompilerParams(vmem_limit_bytes=40 * 2**20),
        cost_estimate=pl.CostEstimate(
            flops=2 * d * tokens * w, bytes_accessed=2 * d * tokens + 4 * d * wide, transcendentals=0
        ),
    )(me.astype(jnp.int32).reshape(1), cot, part)


def shards(hidden, cotangent):
    t, ff = hidden.shape
    tokens, d = cotangent.shape
    groups = tokens // t
    w = ff // groups
    wide = -(-(w + 1) // 128) * 128
    near, far = SIZES["yl"] * SIZES["x"], SIZES["zh"] * SIZES["yh"]
    r = d // (near * far)

    part = lax.all_to_all(
        hidden.T.reshape(groups, w, t), ("chip", "pair"), split_axis=0, concat_axis=0, tiled=True
    )
    cot = cotangent.reshape(tokens, far, near, r).transpose(2, 1, 3, 0).reshape(d, tokens)
    top = jnp.max(jnp.abs(cotangent)).astype(jnp.float32)

    code = code_for(top * jnp.max(jnp.abs(part)).astype(jnp.float32) * tokens)
    lane = jnp.arange(wide) < w

    me = lax.axis_index(("yl", "x"))
    terms, own = product(cot, part, wide, me, near)
    sent = jnp.where(lane, terms * decoded(code), code).astype(jnp.float16)
    got = lax.all_to_all(
        sent.reshape(near, d // near, wide), ("yl", "x"), split_axis=0, concat_axis=0, tiled=True
    )
    back = decoded(-got[:, 0, w].astype(jnp.float32))
    others = (jnp.arange(near) != me)
    weight = jnp.where(others, back, 0.0)[:, None, None]
    row = (got.astype(jnp.float32) * weight).sum(0) + own

    code = code_for(LIMIT * back.sum())
    sent = jnp.where(lane, row * decoded(code), code).astype(jnp.float16)
    got = lax.all_to_all(
        sent.reshape(far, r, wide), ("zh", "yh"), split_axis=0, concat_axis=0, tiled=True
    )
    me = lax.axis_index(("zh", "yh"))
    own = lax.dynamic_slice_in_dim(row, me * r, r, 0)
    back = decoded(-got[:, 0, w].astype(jnp.float32))
    weight = jnp.where(jnp.arange(far) != me, back, 0.0)[:, None, None]
    return ((got.astype(jnp.float32) * weight).sum(0) + own)[:, :w]


def solution(mesh):
    fine = Mesh(mesh.devices.reshape(tuple(SIZES.values())), tuple(SIZES))
    node = ("zh", "yh", "yl", "x")
    in_specs = (P(node + ("chip", "pair"), None), P(node, None))
    out_specs = P(node, ("chip", "pair"))
    return jax.shard_map(shards, mesh=fine, in_specs=in_specs, out_specs=out_specs, check_vma=False)
```

```python
import jax
import jax.numpy as jnp
from jax import lax
from jax.experimental import pallas as pl
from jax.experimental.pallas import tpu as pltpu
from jax.sharding import Mesh, PartitionSpec as P

SIZES = {"zh": 2, "yh": 4, "yl": 2, "x": 4, "chip": 6, "pair": 2}
LIMIT = 60000.0


def decoded(code):
    return jnp.exp2(code)


def code_for(bound):
    e = jnp.floor(jnp.log2(LIMIT) - jnp.log2(jnp.maximum(bound, 1e-30)) - 0.01)
    return jnp.clip(e, -100.0, 100.0)


def multiply(me_ref, cot_ref, part_ref, out_ref, own_ref, flat):
    groups, w, t = part_ref.shape
    step, blocks = pl.program_id(0), out_ref.shape[0] // own_ref.shape[0]

    @pl.when(step == 0)
    def _():
        for i in range(groups):
            flat[i * t:(i + 1) * t, :] = part_ref[i].T

    out_ref[:, :w] = lax.dot_general(
        cot_ref[...], flat[...], (((1,), (0,)), ((), ())), preferred_element_type=jnp.float32
    )
    out_ref[:, w:] = jnp.zeros((out_ref.shape[0], out_ref.shape[1] - w), jnp.float32)

    for i in range(blocks):
        @pl.when(step * blocks + i == me_ref[0])
        def _():
            own_ref[...] = out_ref[i * own_ref.shape[0]:(i + 1) * own_ref.shape[0], :]


def product(cot, part, wide, me, near):
    d, tokens = cot.shape
    groups, w, t = part.shape
    rows = 2 * (d // near)
    return pl.pallas_call(
        multiply,
        grid_spec=pltpu.PrefetchScalarGridSpec(
            num_scalar_prefetch=1,
            grid=(d // rows,),
            in_specs=[
                pl.BlockSpec((rows, tokens), lambda i, _: (i, 0)),
                pl.BlockSpec((groups, w, t), lambda i, _: (0, 0, 0)),
            ],
            out_specs=[
                pl.BlockSpec((rows, wide), lambda i, _: (i, 0)),
                pl.BlockSpec((d // near, wide), lambda i, _: (0, 0)),
            ],
            scratch_shapes=[pltpu.VMEM((tokens, w), jnp.bfloat16)],
        ),
        out_shape=[
            jax.ShapeDtypeStruct((d, wide), jnp.float32),
            jax.ShapeDtypeStruct((d // near, wide), jnp.float32),
        ],
        compiler_params=pltpu.CompilerParams(vmem_limit_bytes=40 * 2**20),
        cost_estimate=pl.CostEstimate(
            flops=2 * d * tokens * w, bytes_accessed=2 * d * tokens + 4 * d * wide, transcendentals=0
        ),
    )(me.astype(jnp.int32).reshape(1), cot, part)


def shards(hidden, cotangent):
    t, ff = hidden.shape
    tokens, d = cotangent.shape
    groups = tokens // t
    w = ff // groups
    wide = -(-(w + 1) // 128) * 128
    near, far = SIZES["yl"] * SIZES["x"], SIZES["zh"] * SIZES["yh"]
    r = d // (near * far)

    part = lax.all_to_all(
        hidden.T.reshape(groups, w, t), ("chip", "pair"), split_axis=0, concat_axis=0, tiled=True
    )
    cot = cotangent.reshape(tokens, far, near, r).transpose(2, 1, 3, 0).reshape(d, tokens)
    top = jnp.max(jnp.abs(cotangent)).astype(jnp.float32)

    code = code_for(top * jnp.max(jnp.abs(part)).astype(jnp.float32) * tokens)
    lane = jnp.arange(wide) < w

    me = lax.axis_index(("yl", "x"))
    terms, own = product(cot, part, wide, me, near)
    sent = jnp.where(lane, terms * decoded(code), code).astype(jnp.float16)
    got = lax.all_to_all(
        sent.reshape(near, d // near, wide), ("yl", "x"), split_axis=0, concat_axis=0, tiled=True
    )
    back = decoded(-got[:, 0, w].astype(jnp.float32))
    others = (jnp.arange(near) != me)
    weight = jnp.where(others, back, 0.0)[:, None, None]
    row = (got.astype(jnp.float32) * weight).sum(0) + own

    code = code_for(LIMIT * back.sum())
    sent = jnp.where(lane, row * decoded(code), code).astype(jnp.float16)
    got = lax.all_to_all(
        sent.reshape(far, r, wide), ("zh", "yh"), split_axis=0, concat_axis=0, tiled=True
    )
    me = lax.axis_index(("zh", "yh"))
    own = lax.dynamic_slice_in_dim(row, me * r, r, 0)
    back = decoded(-got[:, 0, w].astype(jnp.float32))
    weight = jnp.where(jnp.arange(far) != me, back, 0.0)[:, None, None]
    return ((got.astype(jnp.float32) * weight).sum(0) + own)[:, :w]


def solution(mesh):
    fine = Mesh(mesh.devices.reshape(tuple(SIZES.values())), tuple(SIZES))
    node = ("zh", "yh", "yl", "x")
    in_specs = (P(node + ("chip", "pair"), None), P(node, None))
    out_specs = P(node, ("chip", "pair"))
    return jax.shard_map(shards, mesh=fine, in_specs=in_specs, out_specs=out_specs, check_vma=False)
```

```python
import jax
import jax.numpy as jnp
from jax import lax
from jax.experimental import pallas as pl
from jax.experimental.pallas import tpu as pltpu
from jax.sharding import Mesh, PartitionSpec as P

SIZES = {"zh": 2, "yh": 4, "yl": 2, "x": 4, "chip": 6, "pair": 2}
LIMIT = 60000.0


def decoded(code):
    return jnp.exp2(code)


def code_for(bound):
    e = jnp.floor(jnp.log2(LIMIT) - jnp.log2(jnp.maximum(bound, 1e-30)) - 0.01)
    return jnp.clip(e, -100.0, 100.0)


def turn(in_ref, out_ref):
    out_ref[...] = in_ref[...].T


def turned(hidden):
    t, ff = hidden.shape
    piece = ff // 3
    return pl.pallas_call(
        turn,
        grid=(3,),
        in_specs=[pl.BlockSpec((t, piece), lambda i: (0, i))],
        out_specs=pl.BlockSpec((piece, t), lambda i: (i, 0)),
        out_shape=jax.ShapeDtypeStruct((ff, t), hidden.dtype),
        compiler_params=pltpu.CompilerParams(vmem_limit_bytes=40 * 2**20),
    )(hidden)


def multiply(me_ref, cot_ref, part_ref, out_ref, own_ref, flat):
    groups, w, t = part_ref.shape
    step, blocks = pl.program_id(0), out_ref.shape[0] // own_ref.shape[0]

    @pl.when(step == 0)
    def _():
        for i in range(groups):
            flat[:, i * t:(i + 1) * t] = part_ref[i]

    out_ref[:, :w] = lax.dot_general(
        cot_ref[...], flat[...], (((1,), (1,)), ((), ())), preferred_element_type=jnp.float32
    )
    out_ref[:, w:] = jnp.zeros((out_ref.shape[0], out_ref.shape[1] - w), jnp.float32)

    for i in range(blocks):
        @pl.when(step * blocks + i == me_ref[0])
        def _():
            own_ref[...] = out_ref[i * own_ref.shape[0]:(i + 1) * own_ref.shape[0], :]


def product(cot, part, wide, me, near):
    d, tokens = cot.shape
    groups, w, t = part.shape
    rows = 2 * (d // near)
    return pl.pallas_call(
        multiply,
        grid_spec=pltpu.PrefetchScalarGridSpec(
            num_scalar_prefetch=1,
            grid=(d // rows,),
            in_specs=[
                pl.BlockSpec((rows, tokens), lambda i, _: (i, 0)),
                pl.BlockSpec((groups, w, t), lambda i, _: (0, 0, 0)),
            ],
            out_specs=[
                pl.BlockSpec((rows, wide), lambda i, _: (i, 0)),
                pl.BlockSpec((d // near, wide), lambda i, _: (0, 0)),
            ],
            scratch_shapes=[pltpu.VMEM((w, tokens), jnp.bfloat16)],
        ),
        out_shape=[
            jax.ShapeDtypeStruct((d, wide), jnp.float32),
            jax.ShapeDtypeStruct((d // near, wide), jnp.float32),
        ],
        compiler_params=pltpu.CompilerParams(vmem_limit_bytes=40 * 2**20),
        cost_estimate=pl.CostEstimate(
            flops=2 * d * tokens * w, bytes_accessed=2 * d * tokens + 4 * d * wide, transcendentals=0
        ),
    )(me.astype(jnp.int32).reshape(1), cot, part)


def shards(hidden, cotangent):
    t, ff = hidden.shape
    tokens, d = cotangent.shape
    groups = tokens // t
    w = ff // groups
    wide = -(-(w + 1) // 128) * 128
    near, far = SIZES["yl"] * SIZES["x"], SIZES["zh"] * SIZES["yh"]
    r = d // (near * far)

    part = lax.all_to_all(
        turned(hidden).reshape(groups, w, t), ("chip", "pair"), split_axis=0, concat_axis=0, tiled=True
    )
    cot = cotangent.reshape(tokens, far, near, r).transpose(2, 1, 3, 0).reshape(d, tokens)
    top = jnp.max(jnp.abs(cotangent)).astype(jnp.float32)

    code = code_for(top * jnp.max(jnp.abs(part)).astype(jnp.float32) * tokens)
    lane = jnp.arange(wide) < w

    me = lax.axis_index(("yl", "x"))
    terms, own = product(cot, part, wide, me, near)
    sent = jnp.where(lane, terms * decoded(code), code).astype(jnp.float16)
    got = lax.all_to_all(
        sent.reshape(near, d // near, wide), ("yl", "x"), split_axis=0, concat_axis=0, tiled=True
    )
    back = decoded(-got[:, 0, w].astype(jnp.float32))
    others = (jnp.arange(near) != me)
    weight = jnp.where(others, back, 0.0)[:, None, None]
    row = (got.astype(jnp.float32) * weight).sum(0) + own

    code = code_for(LIMIT * back.sum())
    sent = jnp.where(lane, row * decoded(code), code).astype(jnp.float16)
    got = lax.all_to_all(
        sent.reshape(far, r, wide), ("zh", "yh"), split_axis=0, concat_axis=0, tiled=True
    )
    me = lax.axis_index(("zh", "yh"))
    own = lax.dynamic_slice_in_dim(row, me * r, r, 0)
    back = decoded(-got[:, 0, w].astype(jnp.float32))
    weight = jnp.where(jnp.arange(far) != me, back, 0.0)[:, None, None]
    return ((got.astype(jnp.float32) * weight).sum(0) + own)[:, :w]


def solution(mesh):
    fine = Mesh(mesh.devices.reshape(tuple(SIZES.values())), tuple(SIZES))
    node = ("zh", "yh", "yl", "x")
    in_specs = (P(node + ("chip", "pair"), None), P(node, None))
    out_specs = P(node, ("chip", "pair"))
    return jax.shard_map(shards, mesh=fine, in_specs=in_specs, out_specs=out_specs, check_vma=False)
```
